32 devices in a mesh: rep: 2 (over x), tp: 16 (over z, y, core).
Axes of the slice: x: 2, y: 2, z: 4, core: 2. Of those that a mesh axis runs over, the one named last changes fastest.
Arguments:
- tokens: bfloat16 [2, 512, 4096], P(None, 'rep', 'tp'), parts along dimension 1, may hold values from -640 to 640, as said below
- prenorm_gain: bfloat16 [4096], replicated, may hold values from 0.099609375 to 1.8984375
- gate_matrix: bfloat16 [4096, 16384], P(None, 'tp'), may hold values from -0.09375 to 0.09375
- up_weight: bfloat16 [4096, 16384], P(None, 'tp'), may hold values from -0.09375 to 0.09375
- down_weight: bfloat16 [16384, 4096], P('tp'), may hold values from -0.0625 to 0.0625
- a_store: bfloat16 [128, 16, 16384], P('tp'), may hold values from -0.046875 to 0.046875
- b_store: bfloat16 [128, 16, 4096], P('tp'), may hold values from -1.5 to 1.5
- adapter_slot: int32 [256], P('rep'), parts along dimension 0, may hold values from 0 to 127, as said below
- row_adapter: int32 [512], P('rep'), parts along dimension 0, may hold values from 0 to 127, as said below
Outputs:
- mixed: bfloat16 [4096, 2, 512], P('tp', None, 'rep'), parts along dimension 2
The draws below stay inside these ranges and needn't reach their ends.
There are 2 independent parts, one for each index of `rep`. The reference program is written for one: setup_inputs(seed, part) draws one part's arguments, and reference() takes and returns one part's arrays. A program takes and returns all parts, laid end to end along the dimension named above; an argument that names none is the same for every part. Nothing has to cross between parts.
Inputs may be any that keep to these rules, and one draw needn't show every extreme that they name: A permutation: adapter a is stored at index adapter_slot[a] of a_store and b_store, which lies on device adapter_slot[a] // 8 of tp. `row_adapter`: Nondecreasing. Of the adapters that the requests name, at most 2 are stored on one device, and on some device exactly 2. `tokens`: rows and features of different scale.
All inputs are finite; a program needn't handle non-finite values.
Results may differ from the reference program's by a relative error of at most 0.0069.
Values may be sent and summed in bfloat16 or wider, within the bound.
A program may use at most 192 MiB of HBM per device.

```python
import math
import jax
import jax.numpy as jnp
from jax import lax

D = 4096
FF = 16384
RANK = 16
STEPS = 2
ROWS = 256
ADP_DEV = 8
MOST = 2
ADAPTERS = 128


def draw_pair(key):
    k_perm, k_count, k_shift, k_first, k_rows, k_other = jax.random.split(key, 6)
    homes = ADAPTERS // ADP_DEV
    perm = jax.random.permutation(k_perm, ADAPTERS).astype(jnp.int32)
    row_counts = jax.random.randint(k_count, (homes,), 0, MOST + 1).astype(jnp.int32)
    first = jax.random.randint(k_first, (), 0, homes).astype(jnp.int32)
    row_counts = row_counts.at[first].set(MOST)
    order = (jnp.arange(homes, dtype=jnp.int32) + first) % homes
    visited = row_counts[order]
    before = jnp.cumsum(visited) - visited
    kept = jnp.clip(ROWS - before, 0, visited).astype(jnp.int32)
    row_counts = jnp.zeros((homes,), jnp.int32).at[order].set(kept)
    shift = jax.random.randint(k_shift, (homes,), 0, ADP_DEV).astype(jnp.int32)
    local = jnp.arange(ADP_DEV, dtype=jnp.int32)
    used = (local[None, :] + shift[:, None]) % ADP_DEV < row_counts[:, None]
    total = jnp.sum(row_counts)
    used_index = jnp.nonzero(used.reshape(-1), size=ROWS, fill_value=0)[0].astype(jnp.int32)
    inverse = jnp.argsort(perm).astype(jnp.int32)
    pick = jax.random.randint(k_rows, (ROWS,), 0, total).astype(jnp.int32)
    other = jax.random.randint(k_other, (ROWS,), 0, total).astype(jnp.int32)
    pick = jnp.minimum(pick, other)
    position = jnp.arange(ROWS, dtype=jnp.int32)
    pick = jnp.where(position < total, position, pick)
    rows = jnp.sort(inverse[used_index[pick]]).astype(jnp.int32)
    return (perm, rows)


def draw_adapter_slot(key, part):
    shared = draw_pair(key)
    return shared[0]


def draw_row_adapter(key, part):
    shared = draw_pair(key)
    return shared[1]


def draw_tokens(key, part):
    key = jax.random.fold_in(key, 11)
    k_value, k_row, k_col = jax.random.split(key, 3)
    shape = (STEPS, ROWS, D)
    values = jnp.clip(jax.random.normal(k_value, shape, jnp.float32), -4.0, 4.0)
    row_scale = jnp.exp(jax.random.uniform(k_row, (STEPS, ROWS, 1), jnp.float32, 0.0, math.log(10.0)))
    col_scale = jnp.exp(jax.random.uniform(k_col, (D,), jnp.float32, 0.0, math.log(10.0)))
    return (values * row_scale * col_scale).astype(jnp.bfloat16)


def with_spikes(array, key, source, target, shards_of, factor):
    owner, partner = [(jnp.arange(array.shape[axis_at]) // (array.shape[axis_at] // shards_of)).reshape([-1 if axis == axis_at else 1 for axis in range(array.ndim)]) for axis_at in (source, target)]
    chosen = jax.random.permutation(key, shards_of)[partner]
    strong = (owner == chosen) | (owner == (partner + shards_of // 2) % shards_of)
    return jnp.where(strong, factor * array, array)


def steps_of(rng, extent, shards, least, largest):
    def one(dim, blocks):
        draws = jax.random.uniform(jax.random.fold_in(jax.random.fold_in(rng, 6), dim), (blocks,), jnp.float32, least / len(shards), largest / len(shards))
        return jnp.repeat(jnp.exp(draws), extent[dim] // blocks).reshape((-1,) + (1,) * (len(extent) - dim - 1))

    factor_of = one(*shards[0])
    for cut in shards[1:]:
        factor_of = factor_of * one(*cut)
    return factor_of


def normal_values(own_key, extent, width, reach, cuts=(), kind=jnp.bfloat16):
    result = jax.random.normal(own_key, extent, jnp.float32) * width
    if len(cuts) > 0:
        result = steps_of(own_key, extent, cuts, -0.22, 0.18) * result
    return jnp.clip(result, min=-reach, max=reach).astype(kind)


def noise_with(key, dims, deviation, most, pieces, heavy, kind=jnp.bfloat16):
    entries = deviation * jax.random.normal(key, dims, jnp.float32)
    if pieces:
        entries = entries * steps_of(key, dims, pieces, -0.22, 0.18)
    return jnp.clip(with_spikes(entries, jax.random.fold_in(key, 3), *heavy), -most, most).astype(kind)


def setup_inputs(seed: int = 0, part: int = 0) -> dict:
    streams_of = jax.random.split(jax.random.key(seed), 10)
    part_splits = jax.random.split(jax.random.fold_in(streams_of[9], part), 10)
    return {
        "tokens": draw_tokens(jax.random.fold_in(jax.random.fold_in(streams_of[9], part), 71), part),
        "prenorm_gain": jnp.clip(1.0 + 0.18 * jax.random.normal(streams_of[1], (D,), jnp.float32), 0.099609375, 1.8984375).astype(jnp.bfloat16),
        "gate_matrix": normal_values(streams_of[2], (D, FF), D ** -0.5, 0.09375, ((1, 16),)),
        "up_weight": normal_values(streams_of[3], (D, FF), D ** -0.5, 0.09375, ((1, 16),)),
        "down_weight": noise_with(streams_of[4], (FF, D), FF ** -0.5, 0.0625, ((0, 16),), (0, 1, 16, 2.0)),
        "a_store": normal_values(streams_of[5], (ADAPTERS, RANK, FF), FF ** -0.5, 0.046875, ((0, 16),)),
        "b_store": normal_values(streams_of[6], (ADAPTERS, RANK, D), RANK ** -0.5, 1.5, ((0, 16),)),
        "adapter_slot": draw_adapter_slot(jax.random.fold_in(jax.random.fold_in(streams_of[9], part), 71), part),
        "row_adapter": draw_row_adapter(jax.random.fold_in(jax.random.fold_in(streams_of[9], part), 71), part),
    }


def reference(tokens, prenorm_gain, gate_matrix, up_weight, down_weight, a_store, b_store, adapter_slot, row_adapter):
    flat = tokens.astype(jnp.float32).reshape(STEPS * ROWS, D)
    scale = lax.rsqrt(lax.optimization_barrier(jnp.mean(flat * flat, axis=1, keepdims=True)) + 1e-06)
    normed = (flat * scale * prenorm_gain.astype(jnp.float32)).astype(jnp.bfloat16)
    gate = jnp.dot(normed, gate_matrix, preferred_element_type=jnp.float32)
    up = jnp.dot(normed, up_weight, preferred_element_type=jnp.float32)
    hidden = (jax.nn.silu(gate) * up).astype(jnp.bfloat16)
    base_output = jnp.dot(hidden, down_weight, preferred_element_type=jnp.float32)
    slots = jnp.tile(adapter_slot[row_adapter].astype(jnp.int32), STEPS)

    def one_row(pair):
        vector, place = pair
        first = a_store[place]
        second = b_store[place]
        shrink = jnp.dot(first, vector, preferred_element_type=jnp.float32)
        shrink_low = shrink.astype(jnp.bfloat16)
        return jnp.dot(shrink_low, second, preferred_element_type=jnp.float32)
    adapter_delta = lax.map(one_row, (hidden, slots))
    mixed = (base_output + 2.0 * adapter_delta).astype(jnp.bfloat16)
    return mixed.T.reshape(D, STEPS, ROWS)
```

```python
import jax
import jax.numpy as jnp
from jax import lax
from jax.sharding import PartitionSpec as P

EPS = 1e-06
ADAPTER_SCALING = 2.0
MOST = 2


def body(
    tokens,
    prenorm_gain,
    gate_matrix,
    up_weight,
    down_weight,
    a_store,
    b_store,
    adapter_slot,
    row_adapter,
):
    held, rank_count, hidden_all = a_store.shape
    groups = lax.axis_size("tp")
    myself = lax.axis_index("tp")
    stored = groups * held
    catalog = jnp.arange(stored, dtype=jnp.int32)
    matches = row_adapter[:, None] == catalog[None, :]
    row_slot = jnp.sum(jnp.where(matches, adapter_slot[None, :], 0), axis=1)

    home = row_slot // held
    local = row_slot - home * held
    at_home = home[None, :] == jnp.arange(groups, dtype=jnp.int32)[:, None]
    lowest = jnp.min(jnp.where(at_home, local[None, :], held - 1), axis=1)
    highest = jnp.max(jnp.where(at_home, local[None, :], 0), axis=1)
    row_lowest = jnp.sum(jnp.where(at_home, lowest[:, None], 0), axis=0)
    compact = home * MOST + (local != row_lowest).astype(jnp.int32)
    mine_low = lax.dynamic_index_in_dim(lowest, myself, 0, False)
    mine_high = lax.dynamic_index_in_dim(highest, myself, 0, False)

    def chosen(store):
        return jnp.concatenate(
            [
                lax.dynamic_slice_in_dim(store, mine_low, 1, 0),
                lax.dynamic_slice_in_dim(store, mine_high, 1, 0),
            ],
            axis=0,
        )

    whole = lax.all_gather(tokens, "tp", axis=2, tiled=True)
    steps_count, rows_count, width = whole.shape
    total_rows = steps_count * rows_count
    flat = whole.reshape(total_rows, width).astype(jnp.float32)
    scale = lax.rsqrt(jnp.mean(flat * flat, axis=1, keepdims=True) + EPS)
    normed = (flat * scale * prenorm_gain.astype(jnp.float32)).astype(jnp.bfloat16)
    gate = jnp.dot(normed, gate_matrix, preferred_element_type=jnp.float32)
    up = jnp.dot(normed, up_weight, preferred_element_type=jnp.float32)
    hidden = (jax.nn.silu(gate) * up).astype(jnp.bfloat16)

    got_a = lax.all_to_all(chosen(a_store), "tp", split_axis=2, concat_axis=0, tiled=True)
    got_b = lax.all_to_all(chosen(b_store), "tp", split_axis=2, concat_axis=0, tiled=True)
    place_all = jnp.tile(compact, steps_count)
    slot_count = got_a.shape[0]
    chooser = jnp.arange(slot_count, dtype=jnp.int32)[:, None] == place_all[None, :]
    first_flat = got_a.reshape(slot_count * rank_count, got_a.shape[2])
    every_shrink = lax.dot_general(
        first_flat, hidden, (((1,), (1,)), ((), ())), preferred_element_type=jnp.float32
    )
    every_shrink = every_shrink.reshape(slot_count, rank_count, total_rows)
    shrink = jnp.sum(jnp.where(chooser[:, None, :], every_shrink, 0.0), axis=0)
    shrink = lax.psum(shrink, "tp")
    piece = width // groups
    base_output = lax.dot_general(
        down_weight, hidden, (((0,), (1,)), ((), ())), preferred_element_type=jnp.float32
    )
    base_output = lax.psum_scatter(
        base_output.astype(jnp.bfloat16), "tp", scatter_dimension=0, tiled=True
    ).astype(jnp.float32)
    shrink_low = shrink.astype(jnp.bfloat16)
    spread = jnp.where(chooser[:, None, :], shrink_low[None, :, :], jnp.zeros((), jnp.bfloat16))
    spread = spread.reshape(slot_count * rank_count, total_rows)
    second_flat = got_b.reshape(slot_count * rank_count, got_b.shape[2])
    adapter_delta = lax.dot_general(
        second_flat, spread, (((0,), (0,)), ((), ())), preferred_element_type=jnp.float32
    )
    mixed = (base_output + ADAPTER_SCALING * adapter_delta).astype(jnp.bfloat16)
    return mixed.reshape(piece, steps_count, rows_count)


def solution(mesh):
    placed = (
        P(None, "rep", "tp"),
        P(),
        P(None, "tp"),
        P(None, "tp"),
        P("tp", None),
        P("tp", None, None),
        P("tp", None, None),
        P("rep"),
        P("rep"),
    )
    return jax.shard_map(
        body, mesh=mesh, in_specs=placed, out_specs=P("tp", None, "rep"), check_vma=False
    )
```

```python
import functools

import jax
import jax.numpy as jnp
from jax import lax
from jax.experimental import pallas as pl
from jax.experimental.pallas import tpu as pltpu
from jax.sharding import PartitionSpec as P

EPS = 1e-06
ADAPTER_SCALING = 2.0
MOST = 2


def block_kernel(
    n,
    x_ref,
    gain_ref,
    gate_ref,
    up_ref,
    down_ref,
    a_ref,
    b_ref,
    place_ref,
    out_ref,
    gate_v,
    up_v,
    down_v,
    squares,
    normed,
    gate_acc,
    up_acc,
    hidden,
    a_got,
    b_got,
    pair_out,
    pair_in,
    ring_out,
    ring_in,
    fold_out,
    fold_in,
    spread,
    final,
    load_sem,
    sq_send,
    sq_recv,
    ag_send,
    ag_recv,
    sib_send,
    sib_recv,
    a_send,
    a_recv,
    b_send,
    b_recv,
    pair_send,
    pair_recv,
    rs_send,
    rs_recv,
    fold_send,
    fold_recv,
):
    chips = n // 2
    rows, piece = x_ref.shape
    width = n * piece
    units = gate_v.shape[1]
    most_rank = a_ref.shape[0]
    rank = most_rank // MOST
    tile = min(256, units)
    me = lax.axis_index("tp")
    core = me % 2
    chip = me // 2

    def place_of(c):
        z, y = c // 2, c % 2
        return z + y * (chips - 1 - 2 * z)

    def chip_at(place):
        y = place // (chips // 2)
        z = place + y * (chips - 1 - 2 * place)
        return 2 * z + y

    place = place_of(chip)

    def device_at(which_core, back):
        shift = back * (1 - 2 * which_core)
        at = (place - shift + 2 * chips) % chips
        return 2 * chip_at(at) + which_core

    sibling = me + 1 - 2 * core
    other = 1 - core
    following = device_at(core, -1)

    def remote(src, dst, send, recv, to):
        return pltpu.make_async_remote_copy(
            src_ref=src,
            dst_ref=dst,
            send_sem=send,
            recv_sem=recv,
            device_id={"tp": to},
            device_id_type=pl.DeviceIdType.MESH,
        )

    loads = [
        pltpu.make_async_copy(gate_ref, gate_v, load_sem.at[0]),
        pltpu.make_async_copy(up_ref, up_v, load_sem.at[1]),
        pltpu.make_async_copy(down_ref, down_v, load_sem.at[2]),
        pltpu.make_async_copy(
            a_ref.at[:, pl.ds(pl.multiple_of(me * units, 128), units)], a_got.at[0], load_sem.at[3]
        ),
        pltpu.make_async_copy(
            b_ref.at[:, pl.ds(pl.multiple_of(me * piece, 128), piece)], b_got.at[0], load_sem.at[4]
        ),
    ]
    for load in loads:
        load.start()

    barrier = pltpu.get_barrier_semaphore()
    for d in range(1, n):
        pl.semaphore_signal(
            barrier,
            inc=1,
            device_id={"tp": (me + d) % n},
            device_id_type=pl.DeviceIdType.MESH,
        )
    pl.semaphore_wait(barrier, n - 1)

    flat = x_ref[...].astype(jnp.float32)
    partial = jnp.sum(flat * flat, axis=1, keepdims=True)
    turned = jnp.transpose(jnp.broadcast_to(partial, (rows, 128)))
    squares[0] = turned[0:1, :]
    sq = [
        remote(squares.at[0], squares.at[d], sq_send.at[d], sq_recv.at[d], (me + d) % n)
        for d in range(1, n)
    ]
    for copy in sq:
        copy.start()

    def send_adapters(d):
        to = (me + d) % n
        first = remote(
            a_ref.at[:, pl.ds(pl.multiple_of(to * units, 128), units)],
            a_got.at[d],
            a_send.at[d],
            a_recv.at[d],
            to,
        )
        second = remote(
            b_ref.at[:, pl.ds(pl.multiple_of(to * piece, 128), piece)],
            b_got.at[d],
            b_send.at[d],
            b_recv.at[d],
            to,
        )
        first.start()
        second.start()
        return [first, second]

    adapters = {}
    ahead = 4
    for d in range(1, 1 + ahead):
        adapters[d] = send_adapters(d)

    total = squares[0]
    for d in range(1, n):
        sq[d - 1].wait_recv()
        total = total + squares[d]
    scale = lax.rsqrt(total / width + EPS)
    scale = jnp.transpose(jnp.broadcast_to(scale, (128, rows)))
    for c in range(0, piece, 128):
        part = flat[:, c : c + 128] * scale * gain_ref[:, c : c + 128].astype(jnp.float32)
        normed[me, :, c : c + 128] = part.astype(jnp.bfloat16)

    loads[0].wait()
    loads[1].wait()

    def gate_up(device, first):
        at = pl.ds(pl.multiple_of(device * piece, 128), piece)

        @pl.loop(0, units, step=tile)
        def _(start):
            to = pl.ds(pl.multiple_of(start, 128), tile)
            g = jnp.dot(normed[device], gate_v[at, to], preferred_element_type=jnp.float32)
            u = jnp.dot(normed[device], up_v[at, to], preferred_element_type=jnp.float32)
            if first:
                gate_acc[:, to] = g
                up_acc[:, to] = u
            else:
                gate_acc[:, to] += g
                up_acc[:, to] += u

    pending = []
    queue = list(range(1 + ahead, n))
    for s in range(chips):
        mine = device_at(core, s)
        theirs = device_at(other, s)
        if s < chips - 1:
            ring = remote(
                normed.at[mine], normed.at[mine], ag_send.at[s], ag_recv.at[s], following
            )
            ring.start()
            pending.append(ring)
        to_sib = remote(
            normed.at[mine], normed.at[mine], sib_send.at[s], sib_recv.at[s], sibling
        )
        to_sib.start()
        pending.append(to_sib)
        for _ in range(2):
            if queue:
                d = queue.pop(0)
                adapters[d] = send_adapters(d)
        gate_up(mine, s == 0)
        to_sib.wait_recv()
        gate_up(theirs, False)
        if s < chips - 1:
            ring.wait_recv()
    for copy in pending:
        copy.wait_send()
    for copy in sq:
        copy.wait_send()

    @pl.loop(0, units, step=128)
    def _(start):
        to = pl.ds(pl.multiple_of(start, 128), 128)
        g = gate_acc[:, to]
        hidden[:, to] = (g / (1.0 + jnp.exp(-g)) * up_acc[:, to]).astype(jnp.bfloat16)

    loads[2].wait()

    def base(device):
        at = pl.ds(pl.multiple_of(device * piece, 128), piece)
        return jnp.dot(hidden[...], down_v[:, at], preferred_element_type=jnp.float32)

    def chosen(d):
        owner = (me - d + n) % n
        index = lax.broadcasted_iota(jnp.int32, (most_rank, rows), 0) // rank + owner * MOST
        return index == place_ref[...]

    def shrink_partial():
        loads[3].wait()
        loads[4].wait()
        for d in range(1, n):
            adapters[d][0].wait_recv()
            adapters[d][1].wait_recv()

        def add(d, result):
            every = lax.dot_general(
                a_got[d],
                hidden[...],
                (((1,), (1,)), ((), ())),
                preferred_element_type=jnp.float32,
            )
            every = jnp.where(chosen(d), every, 0.0)
            for m in range(MOST):
                result = result + every[m * rank : (m + 1) * rank, :]
            return result

        return lax.fori_loop(0, n, add, jnp.zeros((rank, rows), jnp.float32))

    stages = n.bit_length() - 1
    folds = []

    def fold_start(t):
        bit = 1 << t
        partner = me + bit * (1 - 2 * ((me // bit) % 2))
        copy = remote(
            fold_out.at[t], fold_in.at[t], fold_send.at[t], fold_recv.at[t], partner
        )
        copy.start()
        folds.append(copy)

    def fold_finish(t):
        folds[t].wait_recv()
        return fold_out[t] + fold_in[t]

    pairs = []
    rings = []
    shrink = None
    for s in range(chips):
        pair_out[s] = base(device_at(other, s + 1)).astype(jnp.bfloat16)
        pair = remote(pair_out.at[s], pair_in.at[s], pair_send.at[s], pair_recv.at[s], sibling)
        pair.start()
        pairs.append(pair)
        acc = base(device_at(core, s + 1))
        pair.wait_recv()
        acc = acc + pair_in[s].astype(jnp.float32)
        if s > 0:
            rings[s - 1].wait_recv()
            acc = acc + ring_in[s - 1].astype(jnp.float32)
        if s < chips - 1:
            ring_out[s] = acc.astype(jnp.bfloat16)
            ring = remote(ring_out.at[s], ring_in.at[s], rs_send.at[s], rs_recv.at[s], following)
            ring.start()
            rings.append(ring)
        if s == 0:
            fold_out[0] = shrink_partial()
            fold_start(0)
        elif s <= stages:
            shrink = fold_finish(s - 1)
            if s < stages:
                fold_out[s] = shrink
                fold_start(s)

    low = shrink.astype(jnp.bfloat16).astype(jnp.float32)
    doubled = jnp.concatenate([low] * MOST, axis=0)
    final[...] = acc
    group = 8

    @pl.loop(0, n, step=group)
    def _(first):
        for i in range(group):
            part = jnp.where(chosen(first + i), doubled, 0.0)
            spread[i * most_rank : (i + 1) * most_rank, :] = part
        factors = b_got[pl.ds(first, group)].reshape(group * most_rank, piece)
        left = jnp.transpose(spread[...]).astype(jnp.bfloat16)
        final[...] += ADAPTER_SCALING * jnp.dot(
            left, factors, preferred_element_type=jnp.float32
        )

    out_ref[...] = final[...].astype(out_ref.dtype)

    for copies in adapters.values():
        for copy in copies:
            copy.wait_send()
    for copy in pairs + rings + folds:
        copy.wait_send()


def fused(tokens, prenorm_gain, gate_matrix, up_weight, down_weight, a_sel, b_sel, place_all):
    n = lax.axis_size("tp")
    me = lax.axis_index("tp")
    chips = n // 2
    stages = n.bit_length() - 1
    steps_count, rows_count, piece = tokens.shape
    rows = steps_count * rows_count
    width, units = gate_matrix.shape
    most_rank = a_sel.shape[0]
    rank = most_rank // MOST
    x = tokens.reshape(rows, piece)
    gain = lax.dynamic_slice_in_dim(prenorm_gain, me * piece, piece, 0).reshape(1, piece)
    bf16, f32 = jnp.bfloat16, jnp.float32
    sem = pltpu.SemaphoreType.DMA
    vmem = pl.BlockSpec(memory_space=pltpu.VMEM)
    anywhere = pl.BlockSpec(memory_space=pl.ANY)
    return pl.pallas_call(
        functools.partial(block_kernel, n),
        out_shape=jax.ShapeDtypeStruct((rows, piece), bf16),
        in_specs=[vmem, vmem, anywhere, anywhere, anywhere, anywhere, anywhere, vmem],
        out_specs=vmem,
        scratch_shapes=[
            pltpu.VMEM((width, units), bf16),
            pltpu.VMEM((width, units), bf16),
            pltpu.VMEM((units, width), bf16),
            pltpu.VMEM((n, 1, rows), f32),
            pltpu.VMEM((n, rows, piece), bf16),
            pltpu.VMEM((rows, units), f32),
            pltpu.VMEM((rows, units), f32),
            pltpu.VMEM((rows, units), bf16),
            pltpu.VMEM((n, most_rank, units), bf16),
            pltpu.VMEM((n, most_rank, piece), bf16),
            pltpu.VMEM((chips, rows, piece), bf16),
            pltpu.VMEM((chips, rows, piece), bf16),
            pltpu.VMEM((chips - 1, rows, piece), bf16),
            pltpu.VMEM((chips - 1, rows, piece), bf16),
            pltpu.VMEM((stages, rank, rows), f32),
            pltpu.VMEM((stages, rank, rows), f32),
            pltpu.VMEM((8 * most_rank, rows), f32),
            pltpu.VMEM((rows, piece), f32),
            sem((5,)),
            sem((n,)),
            sem((n,)),
            sem((chips,)),
            sem((chips,)),
            sem((chips,)),
            sem((chips,)),
            sem((n,)),
            sem((n,)),
            sem((n,)),
            sem((n,)),
            sem((chips,)),
            sem((chips,)),
            sem((chips,)),
            sem((chips,)),
            sem((stages,)),
            sem((stages,)),
        ],
        compiler_params=pltpu.CompilerParams(
            collective_id=0, has_side_effects=True, vmem_limit_bytes=58 * 1024 * 1024
        ),
        cost_estimate=pl.CostEstimate(
            flops=6 * rows * width * units, bytes_accessed=6 * width * units, transcendentals=0
        ),
    )(x, gain, gate_matrix, up_weight, down_weight, a_sel, b_sel, place_all.reshape(1, rows))


def fits(n, rows, piece, units, rank):
    held = 3 * n * piece * units * 2 + 8 * rows * units + 2 * n * rows * piece * 2
    return (
        n >= 8
        and n & (n - 1) == 0
        and n.bit_length() - 1 < n // 2
        and n // 2 <= 8
        and rows % 128 == 0
        and piece % 128 == 0
        and units % 128 == 0
        and rank % 16 == 0
        and held < 48 * 1024 * 1024
    )


def body(
    tokens,
    prenorm_gain,
    gate_matrix,
    up_weight,
    down_weight,
    a_store,
    b_store,
    adapter_slot,
    row_adapter,
):
    held, rank_count, hidden_all = a_store.shape
    groups = lax.axis_size("tp")
    myself = lax.axis_index("tp")
    stored = groups * held
    catalog = jnp.arange(stored, dtype=jnp.int32)
    matches = row_adapter[:, None] == catalog[None, :]
    row_slot = jnp.sum(jnp.where(matches, adapter_slot[None, :], 0), axis=1)

    home = row_slot // held
    local = row_slot - home * held
    at_home = home[None, :] == jnp.arange(groups, dtype=jnp.int32)[:, None]
    lowest = jnp.min(jnp.where(at_home, local[None, :], held - 1), axis=1)
    highest = jnp.max(jnp.where(at_home, local[None, :], 0), axis=1)
    row_lowest = jnp.sum(jnp.where(at_home, lowest[:, None], 0), axis=0)
    compact = home * MOST + (local != row_lowest).astype(jnp.int32)
    mine_low = lax.dynamic_index_in_dim(lowest, myself, 0, False)
    mine_high = lax.dynamic_index_in_dim(highest, myself, 0, False)

    def chosen(store):
        return jnp.concatenate(
            [
                lax.dynamic_slice_in_dim(store, mine_low, 1, 0),
                lax.dynamic_slice_in_dim(store, mine_high, 1, 0),
            ],
            axis=0,
        )

    steps_count, rows_count, piece = tokens.shape
    total_rows = steps_count * rows_count
    if fits(groups, total_rows, piece, gate_matrix.shape[1], rank_count):
        mixed = fused(
            tokens,
            prenorm_gain,
            gate_matrix,
            up_weight,
            down_weight,
            chosen(a_store).reshape(MOST * rank_count, hidden_all),
            chosen(b_store).reshape(MOST * rank_count, groups * piece),
            jnp.tile(compact, steps_count),
        )
        return mixed.T.reshape(piece, steps_count, rows_count)

    whole = lax.all_gather(tokens, "tp", axis=2, tiled=True)
    steps_count, rows_count, width = whole.shape
    total_rows = steps_count * rows_count
    flat = whole.reshape(total_rows, width).astype(jnp.float32)
    scale = lax.rsqrt(jnp.mean(flat * flat, axis=1, keepdims=True) + EPS)
    normed = (flat * scale * prenorm_gain.astype(jnp.float32)).astype(jnp.bfloat16)
    gate = jnp.dot(normed, gate_matrix, preferred_element_type=jnp.float32)
    up = jnp.dot(normed, up_weight, preferred_element_type=jnp.float32)
    hidden = (jax.nn.silu(gate) * up).astype(jnp.bfloat16)

    got_a = lax.all_to_all(chosen(a_store), "tp", split_axis=2, concat_axis=0, tiled=True)
    got_b = lax.all_to_all(chosen(b_store), "tp", split_axis=2, concat_axis=0, tiled=True)
    place_all = jnp.tile(compact, steps_count)
    slot_count = got_a.shape[0]
    chooser = jnp.arange(slot_count, dtype=jnp.int32)[:, None] == place_all[None, :]
    first_flat = got_a.reshape(slot_count * rank_count, got_a.shape[2])
    every_shrink = lax.dot_general(
        first_flat, hidden, (((1,), (1,)), ((), ())), preferred_element_type=jnp.float32
    )
    every_shrink = every_shrink.reshape(slot_count, rank_count, total_rows)
    shrink = jnp.sum(jnp.where(chooser[:, None, :], every_shrink, 0.0), axis=0)
    shrink = lax.psum(shrink, "tp")
    piece = width // groups
    base_output = lax.dot_general(
        down_weight, hidden, (((0,), (1,)), ((), ())), preferred_element_type=jnp.float32
    )
    base_output = lax.psum_scatter(
        base_output.astype(jnp.bfloat16), "tp", scatter_dimension=0, tiled=True
    ).astype(jnp.float32)
    shrink_low = shrink.astype(jnp.bfloat16)
    spread = jnp.where(chooser[:, None, :], shrink_low[None, :, :], jnp.zeros((), jnp.bfloat16))
    spread = spread.reshape(slot_count * rank_count, total_rows)
    second_flat = got_b.reshape(slot_count * rank_count, got_b.shape[2])
    adapter_delta = lax.dot_general(
        second_flat, spread, (((0,), (0,)), ((), ())), preferred_element_type=jnp.float32
    )
    mixed = (base_output + ADAPTER_SCALING * adapter_delta).astype(jnp.bfloat16)
    return mixed.reshape(piece, steps_count, rows_count)


def solution(mesh):
    placed = (
        P(None, "rep", "tp"),
        P(),
        P(None, "tp"),
        P(None, "tp"),
        P("tp", None),
        P("tp", None, None),
        P("tp", None, None),
        P("rep"),
        P("rep"),
    )
    return jax.shard_map(
        body, mesh=mesh, in_specs=placed, out_specs=P("tp", None, "rep"), check_vma=False
    )
```

```python
import functools

import jax
import jax.numpy as jnp
from jax import lax
from jax.experimental import pallas as pl
from jax.experimental.pallas import tpu as pltpu
from jax.sharding import PartitionSpec as P

EPS = 1e-06
ADAPTER_SCALING = 2.0
MOST = 2
PARTS = 8


def block_kernel(
    n,
    x_ref,
    gain_ref,
    gate_ref,
    up_ref,
    down_ref,
    a_ref,
    b_ref,
    place_ref,
    out_ref,
    gate_v,
    up_v,
    down_v,
    squares,
    normed,
    gate_acc,
    up_acc,
    hidden,
    a_got,
    b_got,
    pair_out,
    pair_in,
    ring_out,
    ring_in,
    fold_out,
    fold_in,
    spread,
    final,
    load_sem,
    sq_send,
    sq_recv,
    ag_send,
    ag_recv,
    sib_send,
    sib_recv,
    a_send,
    a_recv,
    b_send,
    b_recv,
    pair_send,
    pair_recv,
    rs_send,
    rs_recv,
    fold_send,
    fold_recv,
):
    chips = n // 2
    rows, piece = x_ref.shape
    width = n * piece
    units = gate_v.shape[1]
    most_rank = a_ref.shape[0]
    rank = most_rank // MOST
    tile = min(256, units)
    me = lax.axis_index("tp")
    core = me % 2
    chip = me // 2

    def place_of(c):
        z, y = c // 2, c % 2
        return z + y * (chips - 1 - 2 * z)

    def chip_at(place):
        y = place // (chips // 2)
        z = place + y * (chips - 1 - 2 * place)
        return 2 * z + y

    place = place_of(chip)

    def device_at(which_core, back):
        shift = back * (1 - 2 * which_core)
        at = (place - shift + 2 * chips) % chips
        return 2 * chip_at(at) + which_core

    sibling = me + 1 - 2 * core
    other = 1 - core
    following = device_at(core, -1)

    def remote(src, dst, send, recv, to):
        return pltpu.make_async_remote_copy(
            src_ref=src,
            dst_ref=dst,
            send_sem=send,
            recv_sem=recv,
            device_id={"tp": to},
            device_id_type=pl.DeviceIdType.MESH,
        )

    weights = []
    for w, (source, held) in enumerate(((gate_ref, gate_v), (up_ref, up_v), (down_ref, down_v))):
        share = source.shape[0] // PARTS
        for i in range(PARTS):
            span = pl.ds(i * share, share)
            weights.append(
                pltpu.make_async_copy(
                    source.at[span, :], held.at[span, :], load_sem.at[2 + w * PARTS + i]
                )
            )
    loads = [
        pltpu.make_async_copy(
            a_ref.at[:, pl.ds(pl.multiple_of(me * units, 128), units)], a_got.at[0], load_sem.at[0]
        ),
        pltpu.make_async_copy(
            b_ref.at[:, pl.ds(pl.multiple_of(me * piece, 128), piece)], b_got.at[0], load_sem.at[1]
        ),
    ]
    for load in weights + loads:
        load.start()

    barrier = pltpu.get_barrier_semaphore()
    for d in range(1, n):
        pl.semaphore_signal(
            barrier,
            inc=1,
            device_id={"tp": (me + d) % n},
            device_id_type=pl.DeviceIdType.MESH,
        )
    pl.semaphore_wait(barrier, n - 1)

    flat = x_ref[...].astype(jnp.float32)
    partial = jnp.sum(flat * flat, axis=1, keepdims=True)
    turned = jnp.transpose(jnp.broadcast_to(partial, (rows, 128)))
    squares[0] = turned[0:1, :]
    sq = [
        remote(squares.at[0], squares.at[d], sq_send.at[d], sq_recv.at[d], (me + d) % n)
        for d in range(1, n)
    ]
    for copy in sq:
        copy.start()

    def send_adapters(d):
        to = (me + d) % n
        first = remote(
            a_ref.at[:, pl.ds(pl.multiple_of(to * units, 128), units)],
            a_got.at[d],
            a_send.at[d],
            a_recv.at[d],
            to,
        )
        second = remote(
            b_ref.at[:, pl.ds(pl.multiple_of(to * piece, 128), piece)],
            b_got.at[d],
            b_send.at[d],
            b_recv.at[d],
            to,
        )
        first.start()
        second.start()
        return [first, second]

    adapters = {}
    ahead = 0
    for d in range(1, 1 + ahead):
        adapters[d] = send_adapters(d)

    total = squares[0]
    for d in range(1, n):
        sq[d - 1].wait_recv()
        total = total + squares[d]
    scale = lax.rsqrt(total / width + EPS)
    scale = jnp.transpose(jnp.broadcast_to(scale, (128, rows)))
    for c in range(0, piece, 128):
        part = flat[:, c : c + 128] * scale * gain_ref[
            :, pl.ds(pl.multiple_of(me * piece + c, 128), 128)
        ].astype(jnp.float32)
        normed[me, :, c : c + 128] = part.astype(jnp.bfloat16)

    for load in weights[: 2 * PARTS]:
        load.wait()

    def gate_up(device, first):
        at = pl.ds(pl.multiple_of(device * piece, 128), piece)

        @pl.loop(0, units, step=tile)
        def _(start):
            to = pl.ds(pl.multiple_of(start, 128), tile)
            g = jnp.dot(normed[device], gate_v[at, to], preferred_element_type=jnp.float32)
            u = jnp.dot(normed[device], up_v[at, to], preferred_element_type=jnp.float32)
            if first:
                gate_acc[:, to] = g
                up_acc[:, to] = u
            else:
                gate_acc[:, to] += g
                up_acc[:, to] += u

    pending = []
    queue = list(range(1 + ahead, n))
    for s in range(chips):
        mine = device_at(core, s)
        if s < chips - 1:
            ring = remote(
                normed.at[mine], normed.at[mine], ag_send.at[s], ag_recv.at[s], following
            )
            ring.start()
            pending.append(ring)
        to_sib = remote(
            normed.at[mine], normed.at[mine], sib_send.at[s], sib_recv.at[s], sibling
        )
        to_sib.start()
        pending.append(to_sib)
        for _ in range(2):
            if queue:
                d = queue.pop(0)
                adapters[d] = send_adapters(d)
        if s > 0:
            before.wait_recv()
            gate_up(device_at(other, s - 1), False)
        gate_up(mine, s == 0)
        before = to_sib
        if s < chips - 1:
            ring.wait_recv()
    before.wait_recv()
    gate_up(device_at(other, chips - 1), False)
    for copy in pending:
        copy.wait_send()
    for copy in sq:
        copy.wait_send()

    @pl.loop(0, units, step=128)
    def _(start):
        to = pl.ds(pl.multiple_of(start, 128), 128)
        g = gate_acc[:, to]
        hidden[:, to] = (g / (1.0 + jnp.exp(-g)) * up_acc[:, to]).astype(jnp.bfloat16)

    for load in weights[2 * PARTS :]:
        load.wait()

    def base(device):
        at = pl.ds(pl.multiple_of(device * piece, 128), piece)
        return jnp.dot(hidden[...], down_v[:, at], preferred_element_type=jnp.float32)

    def chosen(d):
        owner = (me - d + n) % n
        index = lax.broadcasted_iota(jnp.int32, (most_rank, rows), 0) // rank + owner * MOST
        return index == place_ref[...]

    def shrink_partial():
        loads[0].wait()
        loads[1].wait()
        for d in range(1, n):
            adapters[d][0].wait_recv()
            adapters[d][1].wait_recv()

        group = n // 2
        half = group * most_rank

        def add(g, result):
            every = lax.dot_general(
                a_got[pl.ds(g * group, group)].reshape(half, units),
                hidden[...],
                (((1,), (1,)), ((), ())),
                preferred_element_type=jnp.float32,
            )
            for i in range(group):
                part = every[i * most_rank : (i + 1) * most_rank, :]
                part = jnp.where(chosen(g * group + i), part, 0.0)
                for m in range(MOST):
                    result = result + part[m * rank : (m + 1) * rank, :]
            return result

        return lax.fori_loop(0, 2, add, jnp.zeros((rank, rows), jnp.float32))

    stages = n.bit_length() - 1
    folds = []

    def fold_start(t):
        bit = 1 << t
        partner = me + bit * (1 - 2 * ((me // bit) % 2))
        copy = remote(
            fold_out.at[t], fold_in.at[t], fold_send.at[t], fold_recv.at[t], partner
        )
        copy.start()
        folds.append(copy)

    def fold_finish(t):
        folds[t].wait_recv()
        return fold_out[t] + fold_in[t]

    pairs = []
    rings = []
    shrink = None
    late = chips - 1 - stages

    def pair_start(s):
        pair_out[s] = base(device_at(other, s + 1)).astype(jnp.bfloat16)
        pair = remote(pair_out.at[s], pair_in.at[s], pair_send.at[s], pair_recv.at[s], sibling)
        pair.start()
        pairs.append(pair)

    pair_start(0)
    for s in range(chips):
        if s < chips - 1:
            pair_start(s + 1)
        acc = base(device_at(core, s + 1))
        pairs[s].wait_recv()
        acc = acc + pair_in[s].astype(jnp.float32)
        if s > 0:
            rings[s - 1].wait_recv()
            acc = acc + ring_in[s - 1].astype(jnp.float32)
        if s < chips - 1:
            ring_out[s] = acc.astype(jnp.bfloat16)
            ring = remote(ring_out.at[s], ring_in.at[s], rs_send.at[s], rs_recv.at[s], following)
            ring.start()
            rings.append(ring)
        t = s - late
        if t == 0:
            fold_out[0] = shrink_partial()
            fold_start(0)
        elif t > 0:
            shrink = fold_finish(t - 1)
            if t < stages:
                fold_out[t] = shrink
                fold_start(t)

    low = shrink.astype(jnp.bfloat16).astype(jnp.float32)
    doubled = jnp.concatenate([low] * MOST, axis=0)
    final[...] = acc
    group = 8

    @pl.loop(0, n, step=group)
    def _(first):
        for i in range(group):
            part = jnp.where(chosen(first + i), doubled, 0.0)
            spread[i * most_rank : (i + 1) * most_rank, :] = part
        factors = b_got[pl.ds(first, group)].reshape(group * most_rank, piece)
        left = jnp.transpose(spread[...]).astype(jnp.bfloat16)
        final[...] += ADAPTER_SCALING * jnp.dot(
            left, factors, preferred_element_type=jnp.float32
        )

    out_ref[...] = final[...].astype(out_ref.dtype)

    for copies in adapters.values():
        for copy in copies:
            copy.wait_send()
    for copy in pairs + rings + folds:
        copy.wait_send()


def select_kernel(n, slot_ref, row_ref, a_ref, b_ref, a_out, b_out, place_ref, sem):
    held, rank, _ = a_ref.shape
    adapters = slot_ref.shape[1]
    rows = row_ref.shape[1]
    me = lax.axis_index("tp")
    slots = jnp.transpose(jnp.broadcast_to(slot_ref[...], (adapters, adapters)))[:, 0:1]
    named = lax.broadcasted_iota(jnp.int32, (adapters, rows), 0) == row_ref[...]
    row_slot = jnp.sum(jnp.where(named, slots, 0), axis=0, keepdims=True)
    home = row_slot // held
    local = row_slot - home * held
    at_home = lax.broadcasted_iota(jnp.int32, (n, rows), 0) == home
    lowest = jnp.min(jnp.where(at_home, local, held - 1), axis=1, keepdims=True)
    row_lowest = jnp.sum(jnp.where(at_home, lowest, 0), axis=0, keepdims=True)
    place = home * MOST + (local != row_lowest).astype(jnp.int32)
    for start in range(0, place_ref.shape[1], rows):
        place_ref[:, start : start + rows] = place
    low = jnp.min(jnp.where(home == me, local, held - 1))
    high = jnp.max(jnp.where(home == me, local, 0))
    copies = []
    for i, at in enumerate((low, high)):
        to = pl.ds(i * rank, rank)
        copies.append(pltpu.make_async_copy(a_ref.at[at], a_out.at[to, :], sem.at[2 * i]))
        copies.append(pltpu.make_async_copy(b_ref.at[at], b_out.at[to, :], sem.at[2 * i + 1]))
    for copy in copies:
        copy.start()
    for copy in copies:
        copy.wait()


def select(adapter_slot, row_adapter, a_store, b_store, steps_count):
    n = lax.axis_size("tp")
    rank = a_store.shape[1]
    rows = row_adapter.shape[0]
    vmem = pl.BlockSpec(memory_space=pltpu.VMEM)
    anywhere = pl.BlockSpec(memory_space=pl.ANY)
    return pl.pallas_call(
        functools.partial(select_kernel, n),
        out_shape=(
            jax.ShapeDtypeStruct((MOST * rank, a_store.shape[2]), a_store.dtype),
            jax.ShapeDtypeStruct((MOST * rank, b_store.shape[2]), b_store.dtype),
            jax.ShapeDtypeStruct((1, steps_count * rows), jnp.int32),
        ),
        in_specs=[vmem, vmem, anywhere, anywhere],
        out_specs=(vmem, vmem, vmem),
        scratch_shapes=[pltpu.SemaphoreType.DMA((2 * MOST,))],
    )(adapter_slot.reshape(1, -1), row_adapter.reshape(1, -1), a_store, b_store)


def fused(tokens, prenorm_gain, gate_matrix, up_weight, down_weight, a_sel, b_sel, place_all):
    n = lax.axis_size("tp")
    chips = n // 2
    stages = n.bit_length() - 1
    steps_count, rows_count, piece = tokens.shape
    rows = steps_count * rows_count
    width, units = gate_matrix.shape
    most_rank = a_sel.shape[0]
    rank = most_rank // MOST
    x = tokens.reshape(rows, piece)
    gain = prenorm_gain.reshape(1, width)
    bf16, f32 = jnp.bfloat16, jnp.float32
    sem = pltpu.SemaphoreType.DMA
    vmem = pl.BlockSpec(memory_space=pltpu.VMEM)
    anywhere = pl.BlockSpec(memory_space=pl.ANY)
    return pl.pallas_call(
        functools.partial(block_kernel, n),
        out_shape=jax.ShapeDtypeStruct((rows, piece), bf16),
        in_specs=[vmem, vmem, anywhere, anywhere, anywhere, vmem, vmem, vmem],
        out_specs=vmem,
        scratch_shapes=[
            pltpu.VMEM((width, units), bf16),
            pltpu.VMEM((width, units), bf16),
            pltpu.VMEM((units, width), bf16),
            pltpu.VMEM((n, 1, rows), f32),
            pltpu.VMEM((n, rows, piece), bf16),
            pltpu.VMEM((rows, units), f32),
            pltpu.VMEM((rows, units), f32),
            pltpu.VMEM((rows, units), bf16),
            pltpu.VMEM((n, most_rank, units), bf16),
            pltpu.VMEM((n, most_rank, piece), bf16),
            pltpu.VMEM((chips, rows, piece), bf16),
            pltpu.VMEM((chips, rows, piece), bf16),
            pltpu.VMEM((chips - 1, rows, piece), bf16),
            pltpu.VMEM((chips - 1, rows, piece), bf16),
            pltpu.VMEM((stages, rank, rows), f32),
            pltpu.VMEM((stages, rank, rows), f32),
            pltpu.VMEM((8 * most_rank, rows), f32),
            pltpu.VMEM((rows, piece), f32),
            sem((2 + 3 * PARTS,)),
            sem((n,)),
            sem((n,)),
            sem((chips,)),
            sem((chips,)),
            sem((chips,)),
            sem((chips,)),
            sem((n,)),
            sem((n,)),
            sem((n,)),
            sem((n,)),
            sem((chips,)),
            sem((chips,)),
            sem((chips,)),
            sem((chips,)),
            sem((stages,)),
            sem((stages,)),
        ],
        compiler_params=pltpu.CompilerParams(
            collective_id=0, has_side_effects=True, vmem_limit_bytes=58 * 1024 * 1024
        ),
        cost_estimate=pl.CostEstimate(
            flops=6 * rows * width * units, bytes_accessed=6 * width * units, transcendentals=0
        ),
    )(x, gain, gate_matrix, up_weight, down_weight, a_sel, b_sel, place_all.reshape(1, rows))


def fits(n, rows, piece, units, rank):
    held = 3 * n * piece * units * 2 + 8 * rows * units + 2 * n * rows * piece * 2
    return (
        n >= 8
        and n & (n - 1) == 0
        and n.bit_length() - 1 < n // 2
        and n // 2 <= 8
        and rows % 256 == 0
        and piece % 128 == 0
        and units % 128 == 0
        and rank % 16 == 0
        and held < 48 * 1024 * 1024
    )


def body(
    tokens,
    prenorm_gain,
    gate_matrix,
    up_weight,
    down_weight,
    a_store,
    b_store,
    adapter_slot,
    row_adapter,
):
    held, rank_count, hidden_all = a_store.shape
    groups = lax.axis_size("tp")
    myself = lax.axis_index("tp")
    steps_count, rows_count, piece = tokens.shape
    total_rows = steps_count * rows_count
    lined = rows_count % 128 == 0 and adapter_slot.shape[0] % 128 == 0
    if lined and fits(groups, total_rows, piece, gate_matrix.shape[1], rank_count):
        a_sel, b_sel, places = select(adapter_slot, row_adapter, a_store, b_store, steps_count)
        mixed = fused(
            tokens, prenorm_gain, gate_matrix, up_weight, down_weight, a_sel, b_sel, places
        )
        return mixed.T.reshape(piece, steps_count, rows_count)

    stored = groups * held
    catalog = jnp.arange(stored, dtype=jnp.int32)
    matches = row_adapter[:, None] == catalog[None, :]
    row_slot = jnp.sum(jnp.where(matches, adapter_slot[None, :], 0), axis=1)

    home = row_slot // held
    local = row_slot - home * held
    at_home = home[None, :] == jnp.arange(groups, dtype=jnp.int32)[:, None]
    lowest = jnp.min(jnp.where(at_home, local[None, :], held - 1), axis=1)
    highest = jnp.max(jnp.where(at_home, local[None, :], 0), axis=1)
    row_lowest = jnp.sum(jnp.where(at_home, lowest[:, None], 0), axis=0)
    compact = home * MOST + (local != row_lowest).astype(jnp.int32)
    mine_low = lax.dynamic_index_in_dim(lowest, myself, 0, False)
    mine_high = lax.dynamic_index_in_dim(highest, myself, 0, False)

    def chosen(store):
        return jnp.concatenate(
            [
                lax.dynamic_slice_in_dim(store, mine_low, 1, 0),
                lax.dynamic_slice_in_dim(store, mine_high, 1, 0),
            ],
            axis=0,
        )

    whole = lax.all_gather(tokens, "tp", axis=2, tiled=True)
    steps_count, rows_count, width = whole.shape
    total_rows = steps_count * rows_count
    flat = whole.reshape(total_rows, width).astype(jnp.float32)
    scale = lax.rsqrt(jnp.mean(flat * flat, axis=1, keepdims=True) + EPS)
    normed = (flat * scale * prenorm_gain.astype(jnp.float32)).astype(jnp.bfloat16)
    gate = jnp.dot(normed, gate_matrix, preferred_element_type=jnp.float32)
    up = jnp.dot(normed, up_weight, preferred_element_type=jnp.float32)
    hidden = (jax.nn.silu(gate) * up).astype(jnp.bfloat16)

    got_a = lax.all_to_all(chosen(a_store), "tp", split_axis=2, concat_axis=0, tiled=True)
    got_b = lax.all_to_all(chosen(b_store), "tp", split_axis=2, concat_axis=0, tiled=True)
    place_all = jnp.tile(compact, steps_count)
    slot_count = got_a.shape[0]
    chooser = jnp.arange(slot_count, dtype=jnp.int32)[:, None] == place_all[None, :]
    first_flat = got_a.reshape(slot_count * rank_count, got_a.shape[2])
    every_shrink = lax.dot_general(
        first_flat, hidden, (((1,), (1,)), ((), ())), preferred_element_type=jnp.float32
    )
    every_shrink = every_shrink.reshape(slot_count, rank_count, total_rows)
    shrink = jnp.sum(jnp.where(chooser[:, None, :], every_shrink, 0.0), axis=0)
    shrink = lax.psum(shrink, "tp")
    piece = width // groups
    base_output = lax.dot_general(
        down_weight, hidden, (((0,), (1,)), ((), ())), preferred_element_type=jnp.float32
    )
    base_output = lax.psum_scatter(
        base_output.astype(jnp.bfloat16), "tp", scatter_dimension=0, tiled=True
    ).astype(jnp.float32)
    shrink_low = shrink.astype(jnp.bfloat16)
    spread = jnp.where(chooser[:, None, :], shrink_low[None, :, :], jnp.zeros((), jnp.bfloat16))
    spread = spread.reshape(slot_count * rank_count, total_rows)
    second_flat = got_b.reshape(slot_count * rank_count, got_b.shape[2])
    adapter_delta = lax.dot_general(
        second_flat, spread, (((0,), (0,)), ((), ())), preferred_element_type=jnp.float32
    )
    mixed = (base_output + ADAPTER_SCALING * adapter_delta).astype(jnp.bfloat16)
    return mixed.reshape(piece, steps_count, rows_count)


def solution(mesh):
    placed = (
        P(None, "rep", "tp"),
        P(),
        P(None, "tp"),
        P(None, "tp"),
        P("tp", None),
        P("tp", None, None),
        P("tp", None, None),
        P("rep"),
        P("rep"),
    )
    return jax.shard_map(
        body, mesh=mesh, in_specs=placed, out_specs=P("tp", None, "rep"), check_vma=False
    )
```
